128 devices in a mesh: row: 8 (over y, core), col: 16 (over z, x).
Axes of the slice: x: 4, y: 4, z: 4, core: 2. Of those that a mesh axis runs over, the one named last changes fastest.
Arguments:
- three_center: bfloat16 [8, 96, 1024, 1024], P('row', 'col'), may hold values from -1 to 1, as said below
- density: bfloat16 [1536, 1536], P('row', 'col'), may hold values from -6 to 6, as said below
- neighbors: int32 [8, 32], P('row'), may hold values from 0 to 47, as said below
- atom_slot: int32 [48], replicated, may hold values from 0 to 47, each once
Outputs:
- exchange: float32 [1536, 1536], P('row', 'col')
The draws below stay inside these ranges and needn't reach their ends.
Inputs may be any that keep to these rules, and one draw needn't show every extreme that they name: `neighbors`: each row lists 32 different atoms, and every atom of the window is listed in some row. `atom_slot`: each storage position holds exactly one atom. Each matrix three_center[a, p] is symmetric. The density matrix is symmetric.
All inputs are finite; a program needn't handle non-finite values.
Results may differ from the reference program's by a relative error of at most 0.0029.
Values may be sent and summed in bfloat16 or wider, within the bound.
No kernel may reach another device: no remote copies, remote signals or barrier semaphores. Data moves between devices by JAX's collectives and lax.ppermute only.
A program may use at most 256 MiB of HBM per device.

```python
import math
import jax
import jax.numpy as jnp
from jax import lax

BS = 32
AB = 96
KN = 32
NA = 48
AUXA = 8


def draw_neighbors(key, part):
    key = jax.random.fold_in(key, 11)
    label_key, order_key = jax.random.split(key)
    labels = jax.random.permutation(label_key, NA)
    starts = jnp.arange(AUXA, dtype=jnp.int32) * (NA // AUXA)
    offsets = jax.vmap(lambda k: jax.random.permutation(k, KN))(jax.random.split(order_key, AUXA))
    places = (starts[:, None] + offsets) % NA
    return labels[places].astype(jnp.int32)


def draw_three_center(key, part):
    key = jax.random.fold_in(key, 21)
    width = KN * BS
    spread = (KN * BS * AB // 4) ** (-0.5)

    def one_atom(sub):
        raw = jax.random.normal(sub, (AB, width, width), jnp.float32)
        sym = (raw + jnp.swapaxes(raw, 1, 2)) * (spread / math.sqrt(2.0))
        return jnp.clip(sym, -1.0, 1.0).astype(jnp.bfloat16)
    return lax.map(one_atom, jax.random.split(key, AUXA))


def draw_density(key, part):
    key = jax.random.fold_in(key, 22)
    total = NA * BS
    main_key = jax.random.fold_in(key, 0)
    raw = jax.random.normal(main_key, (total, total), jnp.float32)
    sym = (raw + raw.T) / math.sqrt(2.0)
    return jnp.clip(sym, -6.0, 6.0).astype(jnp.bfloat16)


def setup_inputs(seed: int = 0) -> dict:
    arg_keys = jax.random.split(jax.random.key(seed), 5)
    return {
        "three_center": draw_three_center(jax.random.fold_in(arg_keys[4], 71), 0),
        "density": draw_density(jax.random.fold_in(arg_keys[4], 71), 0),
        "neighbors": draw_neighbors(jax.random.fold_in(arg_keys[4], 71), 0),
        "atom_slot": jax.random.permutation(arg_keys[3], NA).astype(jnp.int32),
    }


def reference(three_center, density, neighbors, atom_slot):
    slots = jnp.take(atom_slot, neighbors, axis=0).astype(jnp.int32)
    total = NA * BS
    width = KN * BS

    def one_atom(carry, item):
        tensor, slot = item
        rows = jnp.take(density.reshape(NA, BS, total), slot, axis=0).reshape(width, total)
        local = jnp.take(rows.reshape(width, NA, BS), slot, axis=1).reshape(width, width)
        wide = tensor.astype(jnp.float32)
        half = jnp.einsum('pij,jk->pik', wide, local.astype(jnp.float32)).astype(jnp.bfloat16)
        half = lax.optimization_barrier(half).astype(jnp.float32)
        block = jnp.einsum('pik,plk->il', half, wide)
        block = block.reshape(KN, BS, KN, BS).transpose(0, 2, 1, 3)
        carry = carry.at[slot[:, None], :, slot[None, :], :].add(block)
        return carry, None

    start = jnp.zeros((NA, BS, NA, BS), jnp.float32)
    final, _ = lax.scan(one_atom, start, (three_center, slots))
    return final.reshape(total, total)
```

```python
import functools

import jax
import jax.numpy as jnp
from jax import lax
from jax.experimental import pallas as pl
from jax.experimental.pallas import tpu as pltpu
from jax.sharding import PartitionSpec as P

BS = 32
KN = 32
NA = 48
LANES = 128
GB = LANES // BS
NG = KN // GB
ND = NG // 2 + 1
WIDTH = KN * BS
KEEP = ND * LANES
MIB = 1 << 20


def params(mib):
    return pltpu.CompilerParams(vmem_limit_bytes=mib * MIB)


def find(slot_of, nb, storage):
    index = jnp.int32(KN)
    for k in range(KN):
        index = jnp.where(slot_of[nb[0, k]] == storage, k, index)
    return index


def select_kernel(ny, ncol, rows, nb, slot_of, p0, p1, p2, p3, out, panel, chosen, turned):
    row = lax.axis_index("row")
    col = lax.axis_index("col")
    y, h = row // 2, row % 2
    for shift, part in enumerate((p0, p1, p2, p3)):
        owner = lax.rem(y - shift + ny, ny)
        for side in range(2):
            at = (2 * owner + (h if side == 0 else 1 - h)) * rows
            panel[pl.ds(pl.multiple_of(at, 32), rows), :96] = part[side * rows : (side + 1) * rows, :]
    for k in range(KN):
        at = pl.multiple_of(slot_of[nb[0, k]] * BS, BS)
        chosen[k * BS : (k + 1) * BS, :] = panel[pl.ds(at, BS), :]
    for i in range(NG):
        tile = chosen[i * LANES : (i + 1) * LANES, :].T
        turned[:, i * LANES : (i + 1) * LANES] = tile
        if i < ND - 1:
            turned[:, (NG + i) * LANES : (NG + i + 1) * LANES] = tile
    per = NA // ncol
    for j in range(per):
        index = find(slot_of, nb, col * per + j)
        group = jnp.where(index < KN, index // GB, 0)
        start = pl.multiple_of(group * LANES, LANES)
        block = turned[j * BS : (j + 1) * BS, pl.ds(start, KEEP)]
        for i in range(ncol):
            out[i, j * BS : (j + 1) * BS, :] = block


def exchange_kernel(nb, slot_of, gathered, tensor, out, local, half, acc):
    step = pl.program_id(0)
    big = 2 * LANES
    tiles = WIDTH // big

    @pl.when(step == 0)
    def _():
        for k in range(KN):
            at = pl.multiple_of(slot_of[nb[0, k]] * BS, BS)
            group = k // GB
            for d in range(ND):
                to = (group + d) % NG
                local[k * BS : (k + 1) * BS, to * LANES : (to + 1) * LANES] = gathered[
                    pl.ds(at, BS), d * LANES : (d + 1) * LANES
                ]
        for group in range(NG):
            for d in range(1, NG // 2):
                to = (group + d) % NG
                local[to * LANES : (to + 1) * LANES, group * LANES : (group + 1) * LANES] = local[
                    group * LANES : (group + 1) * LANES, to * LANES : (to + 1) * LANES
                ].T
        acc[...] = jnp.zeros_like(acc)

    for i in range(tiles):
        half[i * big : (i + 1) * big, :] = jnp.dot(
            local[i * big : (i + 1) * big, :], tensor[0], preferred_element_type=jnp.float32
        ).astype(jnp.bfloat16)
    for i in range(tiles):
        left = tensor[0, i * big : (i + 1) * big, :]
        first = min(tiles - 1, tiles - i)
        acc[i, :, : first * big] += jnp.dot(
            left, half[:, i * big : (i + first) * big], preferred_element_type=jnp.float32
        )
        if first < tiles - 1:
            acc[i, :, first * big :] += jnp.dot(
                left, half[:, : (tiles - 1 - first) * big], preferred_element_type=jnp.float32
            )

    @pl.when(step == pl.num_programs(0) - 1)
    def _():
        ncol = lax.axis_size("col")
        scale = 1.0 + lax.axis_index("col").astype(jnp.float32) / ncol
        out[...] = jnp.zeros_like(out)
        for k in range(KN):
            at = pl.multiple_of(slot_of[nb[0, k]] * BS, BS)
            group = k // GB
            i, odd = group // 2, group % 2
            r = (k % (2 * GB)) * BS
            piece = acc[i, r : r + BS, odd * LANES : odd * LANES + KEEP]
            out[pl.ds(at, BS), :] = (piece * scale).astype(jnp.bfloat16)


def place_kernel(ny, ncol, rows, nb, slot_of, parts, mine, other, total, turned, placed):
    row = lax.axis_index("row")
    col = lax.axis_index("col")
    y, h = row // 2, row % 2
    per = NA // ncol
    sums = parts[0].astype(jnp.float32)
    for i in range(1, ncol):
        sums += parts[i].astype(jnp.float32) * (1.0 / (1.0 + i / ncol))
    total[:96, :] = sums
    for d in range(ND):
        tile = total[:, d * LANES : (d + 1) * LANES].T
        turned[d * LANES : (d + 1) * LANES, :] = tile * 0.5 if d in (0, NG // 2) else tile
    placed[...] = jnp.zeros_like(placed)
    for j in range(per):
        index = find(slot_of, nb, col * per + j)

        @pl.when(index < KN)
        def _():
            group = index // GB
            for d in range(ND):
                to = lax.rem(group + d, NG)
                for b in range(GB):
                    at = pl.multiple_of(slot_of[nb[0, to * GB + b]] * BS, BS)
                    r = d * LANES + b * BS
                    placed[pl.ds(at, BS), j * BS : (j + 1) * BS] = turned[
                        r : r + BS, j * BS : (j + 1) * BS
                    ]

    for shift in range(ny):
        owner = lax.rem(y + shift, ny)
        at = pl.multiple_of((2 * owner + h) * rows, 32)
        mine[shift] = placed[pl.ds(at, rows), :]
        at = pl.multiple_of((2 * owner + 1 - h) * rows, 32)
        other[shift] = placed[pl.ds(at, rows), :]


def mirror_kernel(part, direct, first, second, out):
    b = lax.axis_index("col") % 2
    for side, block in ((b, first), (1 - b, second)):
        at = pl.multiple_of(side * part, 32)
        out[pl.ds(at, part), :] = direct[pl.ds(at, part), :] + block[...].T


VMEM = pl.BlockSpec(memory_space=pltpu.VMEM)
SMEM = pl.BlockSpec(memory_space=pltpu.SMEM)


def shards(three_center, density, neighbors, atom_slot):
    nrow = lax.axis_size("row")
    ncol = lax.axis_size("col")
    ny = nrow // 2
    rows, cols = density.shape
    total = NA * BS
    core = [(i, i ^ 1) for i in range(nrow)]

    def along(k):
        return [(i, (i + 2 * k) % nrow) for i in range(nrow)]

    pair = jnp.concatenate([density, lax.ppermute(density, "row", core)], axis=0)
    others = [lax.ppermute(pair, "row", along(k)) for k in range(1, ny)]
    copies = pl.pallas_call(
        functools.partial(select_kernel, ny, ncol, rows),
        out_shape=jax.ShapeDtypeStruct((ncol, cols, KEEP), jnp.bfloat16),
        in_specs=[SMEM, SMEM] + [VMEM] * 4,
        out_specs=VMEM,
        scratch_shapes=[
            pltpu.VMEM((total, LANES), jnp.bfloat16),
            pltpu.VMEM((WIDTH, LANES), jnp.bfloat16),
            pltpu.VMEM((LANES, WIDTH + KEEP - LANES), jnp.bfloat16),
        ],
        compiler_params=params(24),
        name="select",
    )(neighbors, atom_slot, pair, *others)
    gathered = lax.all_to_all(copies, "col", 0, 0, tiled=True).reshape(total, KEEP)
    tensor = three_center[0]
    nfun = tensor.shape[0]
    sent = pl.pallas_call(
        exchange_kernel,
        out_shape=jax.ShapeDtypeStruct((total, KEEP), jnp.bfloat16),
        grid=(nfun,),
        in_specs=[
            SMEM,
            SMEM,
            pl.BlockSpec((total, KEEP), lambda p: (0, 0)),
            pl.BlockSpec((1, WIDTH, WIDTH), lambda p: (p, 0, 0)),
        ],
        out_specs=pl.BlockSpec((total, KEEP), lambda p: (0, 0)),
        scratch_shapes=[
            pltpu.VMEM((WIDTH, WIDTH), jnp.bfloat16),
            pltpu.VMEM((WIDTH, WIDTH), jnp.bfloat16),
            pltpu.VMEM((4, 2 * LANES, 6 * LANES), jnp.float32),
        ],
        compiler_params=params(48),
        name="exchange",
    )(neighbors, atom_slot, gathered, tensor)
    parts = lax.all_to_all(sent.reshape(ncol, cols, KEEP), "col", 0, 0, tiled=True)
    mine, other = pl.pallas_call(
        functools.partial(place_kernel, ny, ncol, rows),
        out_shape=[jax.ShapeDtypeStruct((ny, rows, cols), jnp.float32)] * 2,
        in_specs=[SMEM, SMEM, VMEM],
        out_specs=[VMEM, VMEM],
        scratch_shapes=[
            pltpu.VMEM((LANES, KEEP), jnp.float32),
            pltpu.VMEM((KEEP, LANES), jnp.float32),
            pltpu.VMEM((total, cols), jnp.float32),
        ],
        compiler_params=params(24),
        name="place",
    )(neighbors, atom_slot, parts)
    chip = mine + lax.ppermute(other, "row", core)
    direct = chip[0]
    for k in range(1, ny):
        direct = direct + lax.ppermute(chip[k], "row", along(k))
    half = rows // 2
    b = lax.axis_index("col") % 2
    same = [(R * ncol + C, (C // 2) * ncol + 2 * R + C % 2) for R in range(nrow) for C in range(ncol)]
    swap = [(R * ncol + C, (C // 2) * ncol + 2 * R + 1 - C % 2) for R in range(nrow) for C in range(ncol)]
    upper, lower = direct[:half], direct[half:]
    first = lax.ppermute(jnp.where(b == 0, upper, lower), ("row", "col"), same)
    second = lax.ppermute(jnp.where(b == 0, lower, upper), ("row", "col"), swap)
    return pl.pallas_call(
        functools.partial(mirror_kernel, half),
        out_shape=jax.ShapeDtypeStruct((rows, cols), jnp.float32),
        in_specs=[VMEM] * 3,
        out_specs=VMEM,
        name="mirror",
    )(direct, first, second)


def solution(mesh):
    placed = (P("row", "col", None, None), P("row", "col"), P("row", None), P())
    return jax.shard_map(
        shards, mesh=mesh, in_specs=placed, out_specs=P("row", "col"), check_vma=False
    )
```

```python
import functools
import math

import jax
import jax.numpy as jnp
from jax import lax
from jax.experimental import pallas as pl
from jax.experimental.pallas import tpu as pltpu
from jax.sharding import PartitionSpec as P

BS = 32
KN = 32
NA = 48
LANES = 128
GB = LANES // BS
NG = KN // GB
ND = NG // 2 + 1
WIDTH = KN * BS
KEEP = ND * LANES
MIB = 1 << 20


def params(mib):
    return pltpu.CompilerParams(vmem_limit_bytes=mib * MIB)


def find(slot_of, nb, storage):
    index = jnp.int32(KN)
    for k in range(KN):
        index = jnp.where(slot_of[nb[0, k]] == storage, k, index)
    return index


def select_kernel(ny, ncol, rows, nb, slot_of, p0, p1, p2, p3, out, panel, chosen, turned, sem):
    row = lax.axis_index("row")
    col = lax.axis_index("col")
    y, h = row // 2, row % 2
    copies = []
    for shift, part in enumerate((p0, p1, p2, p3)):
        owner = lax.rem(y - shift + ny, ny)
        for side in range(2):
            at = pl.multiple_of((2 * owner + (h if side == 0 else 1 - h)) * rows, 32)
            copies.append(
                pltpu.make_async_copy(
                    part.at[pl.ds(side * rows, rows), :],
                    panel.at[pl.ds(at, rows), :],
                    sem.at[2 * shift + side],
                )
            )
    for copy in copies:
        copy.start()
    for copy in copies:
        copy.wait()
    for k in range(KN):
        at = pl.multiple_of(slot_of[nb[0, k]] * BS, BS)
        chosen[k * BS : (k + 1) * BS, :96] = panel[pl.ds(at, BS), :]
    for i in range(NG):
        tile = chosen[i * LANES : (i + 1) * LANES, :].T
        turned[:, i * LANES : (i + 1) * LANES] = tile
        if i < ND - 1:
            turned[:, (NG + i) * LANES : (NG + i + 1) * LANES] = tile
    per = NA // ncol
    for j in range(per):
        index = find(slot_of, nb, col * per + j)
        group = jnp.where(index < KN, index // GB, 0)
        start = pl.multiple_of(group * LANES, LANES)
        out[j * BS : (j + 1) * BS, :] = turned[j * BS : (j + 1) * BS, pl.ds(start, KEEP)]


def exchange_kernel(side, q0, q1, q2, q3, nb, slot_of, tensor, out, gathered, local, half, acc):
    step = pl.program_id(0)
    big = 2 * LANES
    tiles = WIDTH // big

    @pl.when(step == 0)
    def _():
        h = lax.axis_index("row") % 2
        z, x = lax.axis_index("col") // side, lax.axis_index("col") % side
        cols = gathered.shape[0] // side**2
        for j, part in enumerate((q0, q1, q2, q3)):
            for k in range(side):
                dz, dx = jnp.where(h == 0, j, k), jnp.where(h == 0, k, j)
                owner = lax.rem(z - dz + side, side) * side + lax.rem(x - dx + side, side)
                at = pl.multiple_of(owner * cols, 32)
                gathered[pl.ds(at, cols), :] = part[k * cols : (k + 1) * cols, :]
        for k in range(KN):
            at = pl.multiple_of(slot_of[nb[0, k]] * BS, BS)
            group = k // GB
            for d in range(ND):
                to = (group + d) % NG
                local[k * BS : (k + 1) * BS, to * LANES : (to + 1) * LANES] = gathered[
                    pl.ds(at, BS), d * LANES : (d + 1) * LANES
                ]
        for group in range(NG):
            for d in range(1, NG // 2):
                to = (group + d) % NG
                local[to * LANES : (to + 1) * LANES, group * LANES : (group + 1) * LANES] = local[
                    group * LANES : (group + 1) * LANES, to * LANES : (to + 1) * LANES
                ].T
        acc[...] = jnp.zeros_like(acc)

    for i in range(tiles):
        half[i * big : (i + 1) * big, :] = jnp.dot(
            local[i * big : (i + 1) * big, :], tensor[0], preferred_element_type=jnp.float32
        ).astype(jnp.bfloat16)
    for i in range(tiles):
        left = tensor[0, i * big : (i + 1) * big, :]
        first = min(tiles - 1, tiles - i)
        acc[i, :, : first * big] += jnp.dot(
            left, half[:, i * big : (i + first) * big], preferred_element_type=jnp.float32
        )
        if first < tiles - 1:
            acc[i, :, first * big :] += jnp.dot(
                left, half[:, : (tiles - 1 - first) * big], preferred_element_type=jnp.float32
            )

    @pl.when(step == pl.num_programs(0) - 1)
    def _():
        ncol = lax.axis_size("col")
        scale = 1.0 + lax.axis_index("col").astype(jnp.float32) / ncol
        out[...] = jnp.zeros_like(out)
        for k in range(KN):
            at = pl.multiple_of(slot_of[nb[0, k]] * BS, BS)
            group = k // GB
            i, odd = group // 2, group % 2
            r = (k % (2 * GB)) * BS
            piece = acc[i, r : r + BS, odd * LANES : odd * LANES + KEEP]
            out[pl.ds(at, BS), :] = (piece * scale).astype(jnp.bfloat16)


def place_kernel(ny, ncol, rows, nb, slot_of, parts, mine, other, total, turned, placed):
    row = lax.axis_index("row")
    col = lax.axis_index("col")
    y, h = row // 2, row % 2
    per = NA // ncol
    sums = parts[0].astype(jnp.float32)
    for i in range(1, ncol):
        sums += parts[i].astype(jnp.float32) * (1.0 / (1.0 + i / ncol))
    total[:96, :] = sums
    for d in range(ND):
        tile = total[:, d * LANES : (d + 1) * LANES].T
        turned[d * LANES : (d + 1) * LANES, :] = tile * 0.5 if d in (0, NG // 2) else tile
    placed[...] = jnp.zeros_like(placed)
    for j in range(per):
        index = find(slot_of, nb, col * per + j)

        @pl.when(index < KN)
        def _():
            group = index // GB
            for d in range(ND):
                to = lax.rem(group + d, NG)
                for b in range(GB):
                    at = pl.multiple_of(slot_of[nb[0, to * GB + b]] * BS, BS)
                    r = d * LANES + b * BS
                    placed[pl.ds(at, BS), j * BS : (j + 1) * BS] = turned[
                        r : r + BS, j * BS : (j + 1) * BS
                    ]

    for shift in range(ny):
        owner = lax.rem(y + shift, ny)
        at = pl.multiple_of((2 * owner + h) * rows, 32)
        mine[shift] = placed[pl.ds(at, rows), :]
        at = pl.multiple_of((2 * owner + 1 - h) * rows, 32)
        other[shift] = placed[pl.ds(at, rows), :]


def mirror_kernel(part, direct, first, second, out):
    b = lax.axis_index("col") % 2
    for side, block in ((b, first), (1 - b, second)):
        at = pl.multiple_of(side * part, 32)
        out[pl.ds(at, part), :] = direct[pl.ds(at, part), :] + block[...].T


VMEM = pl.BlockSpec(memory_space=pltpu.VMEM)
SMEM = pl.BlockSpec(memory_space=pltpu.SMEM)
ANY = pl.BlockSpec(memory_space=pl.ANY)


def shards(three_center, density, neighbors, atom_slot):
    nrow = lax.axis_size("row")
    ncol = lax.axis_size("col")
    ny = nrow // 2
    rows, cols = density.shape
    total = NA * BS
    core = [(i, i ^ 1) for i in range(nrow)]

    def along(k):
        return [(i, (i + 2 * k) % nrow) for i in range(nrow)]

    pair = jnp.concatenate([density, lax.ppermute(density, "row", core)], axis=0)
    others = [lax.ppermute(pair, "row", along(k)) for k in range(1, ny)]
    block = pl.pallas_call(
        functools.partial(select_kernel, ny, ncol, rows),
        out_shape=jax.ShapeDtypeStruct((cols, KEEP), jnp.bfloat16),
        in_specs=[SMEM, SMEM] + [ANY] * 4,
        out_specs=VMEM,
        scratch_shapes=[
            pltpu.VMEM((total, cols), jnp.bfloat16),
            pltpu.VMEM((WIDTH, LANES), jnp.bfloat16),
            pltpu.VMEM((LANES, WIDTH + KEEP - LANES), jnp.bfloat16),
            pltpu.SemaphoreType.DMA((2 * ny,)),
        ],
        compiler_params=params(12),
        name="select",
    )(neighbors, atom_slot, pair, *others)
    side = math.isqrt(ncol)

    def stage(k, first):
        pairs = []
        for r in range(nrow):
            for c in range(ncol):
                z, x = divmod(c, side)
                if (r % 2 == 0) == first:
                    x = (x + k) % side
                else:
                    z = (z + k) % side
                pairs.append((r * ncol + c, r * ncol + z * side + x))
        return pairs

    both = ("row", "col")
    line = [block] + [lax.ppermute(block, both, stage(k, True)) for k in range(1, side)]
    line = jnp.concatenate(line, axis=0)
    plane = [line] + [lax.ppermute(line, both, stage(k, False)) for k in range(1, side)]
    tensor = three_center[0]
    nfun = tensor.shape[0]
    sent = pl.pallas_call(
        functools.partial(exchange_kernel, side),
        out_shape=jax.ShapeDtypeStruct((total, KEEP), jnp.bfloat16),
        grid=(nfun,),
        in_specs=[pl.BlockSpec(line.shape, lambda p: (0, 0))] * side
        + [
            SMEM,
            SMEM,
            pl.BlockSpec((1, WIDTH, WIDTH), lambda p: (p, 0, 0)),
        ],
        out_specs=pl.BlockSpec((total, KEEP), lambda p: (0, 0)),
        scratch_shapes=[
            pltpu.VMEM((total, KEEP), jnp.bfloat16),
            pltpu.VMEM((WIDTH, WIDTH), jnp.bfloat16),
            pltpu.VMEM((WIDTH, WIDTH), jnp.bfloat16),
            pltpu.VMEM((4, 2 * LANES, 6 * LANES), jnp.float32),
        ],
        compiler_params=params(48),
        name="exchange",
    )(*plane, neighbors, atom_slot, tensor)
    parts = lax.all_to_all(sent.reshape(ncol, cols, KEEP), "col", 0, 0, tiled=True)
    mine, other = pl.pallas_call(
        functools.partial(place_kernel, ny, ncol, rows),
        out_shape=[jax.ShapeDtypeStruct((ny, rows, cols), jnp.float32)] * 2,
        in_specs=[SMEM, SMEM, VMEM],
        out_specs=[VMEM, VMEM],
        scratch_shapes=[
            pltpu.VMEM((LANES, KEEP), jnp.float32),
            pltpu.VMEM((KEEP, LANES), jnp.float32),
            pltpu.VMEM((total, cols), jnp.float32),
        ],
        compiler_params=params(12),
        name="place",
    )(neighbors, atom_slot, parts)
    chip = mine + lax.ppermute(other, "row", core)
    direct = chip[0]
    for k in range(1, ny):
        direct = direct + lax.ppermute(chip[k], "row", along(k))
    half = rows // 2
    b = lax.axis_index("col") % 2
    same = [(R * ncol + C, (C // 2) * ncol + 2 * R + C % 2) for R in range(nrow) for C in range(ncol)]
    swap = [(R * ncol + C, (C // 2) * ncol + 2 * R + 1 - C % 2) for R in range(nrow) for C in range(ncol)]
    upper, lower = direct[:half], direct[half:]
    first = lax.ppermute(jnp.where(b == 0, upper, lower), ("row", "col"), same)
    second = lax.ppermute(jnp.where(b == 0, lower, upper), ("row", "col"), swap)
    return pl.pallas_call(
        functools.partial(mirror_kernel, half),
        out_shape=jax.ShapeDtypeStruct((rows, cols), jnp.float32),
        in_specs=[VMEM] * 3,
        out_specs=VMEM,
        compiler_params=params(12),
        name="mirror",
    )(direct, first, second)


def solution(mesh):
    placed = (P("row", "col", None, None), P("row", "col"), P("row", None), P())
    return jax.shard_map(
        shards, mesh=mesh, in_specs=placed, out_specs=P("row", "col"), check_vma=False
    )
```

```python
import functools
import math

import jax
import jax.numpy as jnp
from jax import lax
from jax.experimental import pallas as pl
from jax.experimental.pallas import tpu as pltpu
from jax.sharding import PartitionSpec as P

BS = 32
KN = 32
NA = 48
LANES = 128
GB = LANES // BS
NG = KN // GB
ND = NG // 2 + 1
WIDTH = KN * BS
KEEP = ND * LANES
FAR = (ND - 1) * LANES
HB = BS // 2
PANEL = 3 * (BS * (ND - 1) + HB)
TAIL = 3 * BS * (ND - 1)
MIB = 1 << 20


def params(mib):
    return pltpu.CompilerParams(vmem_limit_bytes=mib * MIB)


def find(slot_of, nb, storage):
    index = jnp.int32(KN)
    for k in range(KN):
        index = jnp.where(slot_of[nb[0, k]] == storage, k, index)
    return index


def far_half(index):
    late = (index // (KN // 2)) % 2
    upper = (index % GB) // (GB // 2)
    return (upper + late) % 2


def pack_far(tile, half):
    turn = pltpu.roll(tile, LANES // 2, 1)
    left = lax.broadcasted_iota(jnp.int32, (HB, LANES), 1) < LANES // 2
    low = jnp.where(half == 0, tile, turn)[:HB]
    high = jnp.where(half == 0, turn, tile)[HB:]
    return jnp.where(left, low, high)


def unpack_far(packed):
    return jnp.concatenate([packed, pltpu.roll(packed, LANES // 2, 1)], axis=0)


def select_kernel(ny, ncol, rows, nb, slot_of, p0, p1, p2, p3, out, panel, chosen, turned, sem):
    row = lax.axis_index("row")
    col = lax.axis_index("col")
    y, h = row // 2, row % 2
    copies = []
    for shift, part in enumerate((p0, p1, p2, p3)):
        owner = lax.rem(y - shift + ny, ny)
        for side in range(2):
            at = pl.multiple_of((2 * owner + (h if side == 0 else 1 - h)) * rows, 32)
            copies.append(
                pltpu.make_async_copy(
                    part.at[pl.ds(side * rows, rows), :],
                    panel.at[pl.ds(at, rows), :],
                    sem.at[2 * shift + side],
                )
            )
    for copy in copies:
        copy.start()
    for copy in copies:
        copy.wait()
    for k in range(KN):
        at = pl.multiple_of(slot_of[nb[0, k]] * BS, BS)
        chosen[k * BS : (k + 1) * BS, :96] = panel[pl.ds(at, BS), :]
    for i in range(NG):
        tile = chosen[i * LANES : (i + 1) * LANES, :].T
        turned[:, i * LANES : (i + 1) * LANES] = tile
        if i < ND - 1:
            turned[:, (NG + i) * LANES : (NG + i + 1) * LANES] = tile
    per = NA // ncol
    for j in range(per):
        index = find(slot_of, nb, col * per + j)
        group = jnp.where(index < KN, index // GB, 0)
        start = pl.multiple_of(group * LANES, LANES)
        lines = turned[j * BS : (j + 1) * BS, pl.ds(start, KEEP)]
        for d in range(ND - 1):
            r = (d * per + j) * BS
            out[r : r + BS, :] = lines[:, d * LANES : (d + 1) * LANES]
        far = pack_far(lines[:, FAR:].astype(jnp.float32), far_half(index))
        out[TAIL + j * HB : TAIL + (j + 1) * HB, :] = far.astype(jnp.bfloat16)


def place_of(storage):
    return (storage // 3) * PANEL, storage % 3


def exchange_kernel(side, q0, q1, q2, q3, nb, slot_of, tensor, out, gathered, local, half, acc):
    step = pl.program_id(0)
    big = 2 * LANES
    tiles = WIDTH // big

    @pl.when(step == 0)
    def _():
        h = lax.axis_index("row") % 2
        z, x = lax.axis_index("col") // side, lax.axis_index("col") % side
        left = lax.broadcasted_iota(jnp.int32, (BS, LANES), 1) < LANES // 2
        for j, part in enumerate((q0, q1, q2, q3)):
            for k in range(side):
                dz, dx = jnp.where(h == 0, j, k), jnp.where(h == 0, k, j)
                owner = lax.rem(z - dz + side, side) * side + lax.rem(x - dx + side, side)
                at = pl.multiple_of(owner * PANEL, 16)
                gathered[pl.ds(at, PANEL), :] = part[k * PANEL : (k + 1) * PANEL, :]
        for k in range(KN):
            base, j = place_of(slot_of[nb[0, k]])
            group = k // GB
            for d in range(ND - 1):
                to = (group + d) % NG
                at = pl.multiple_of(base + (d * 3 + j) * BS, 16)
                local[k * BS : (k + 1) * BS, to * LANES : (to + 1) * LANES] = gathered[pl.ds(at, BS), :]
            at = pl.multiple_of(base + TAIL + j * HB, 16)
            tile = unpack_far(gathered[pl.ds(at, HB), :].astype(jnp.float32))
            if far_half(k):
                tile = jnp.where(left, 0.0, pltpu.roll(tile, LANES // 2, 1))
            else:
                tile = jnp.where(left, tile, 0.0)
            to = (group + NG // 2) % NG
            local[k * BS : (k + 1) * BS, to * LANES : (to + 1) * LANES] = tile.astype(jnp.bfloat16)
        for group in range(NG):
            here = slice(group * LANES, (group + 1) * LANES)
            for d in range(1, NG // 2):
                to = (group + d) % NG
                there = slice(to * LANES, (to + 1) * LANES)
                local[there, here] = local[here, there].T
        for group in range(NG // 2):
            here = slice(group * LANES, (group + 1) * LANES)
            there = slice((group + NG // 2) * LANES, (group + NG // 2 + 1) * LANES)
            tile = local[here, there] + local[there, here].T
            local[here, there] = tile
            local[there, here] = tile.T
        acc[...] = jnp.zeros_like(acc)

    for i in range(tiles):
        half[i * big : (i + 1) * big, :] = jnp.dot(
            local[i * big : (i + 1) * big, :], tensor[0], preferred_element_type=jnp.float32
        ).astype(jnp.bfloat16)
    for i in range(tiles):
        left = tensor[0, i * big : (i + 1) * big, :]
        first = min(tiles - 1, tiles - i)
        acc[i, :, : first * big] += jnp.dot(
            left, half[:, i * big : (i + first) * big], preferred_element_type=jnp.float32
        )
        if first < tiles - 1:
            acc[i, :, first * big :] += jnp.dot(
                left, half[:, : (tiles - 1 - first) * big], preferred_element_type=jnp.float32
            )

    @pl.when(step == pl.num_programs(0) - 1)
    def _():
        ncol = lax.axis_size("col")
        scale = 1.0 + lax.axis_index("col").astype(jnp.float32) / ncol
        out[...] = jnp.zeros_like(out)
        for k in range(KN):
            base, j = place_of(slot_of[nb[0, k]])
            group = k // GB
            i, odd = group // 2, group % 2
            r = (k % (2 * GB)) * BS
            piece = acc[i, r : r + BS, odd * LANES : odd * LANES + KEEP] * scale
            for d in range(ND - 1):
                at = pl.multiple_of(base + (d * 3 + j) * BS, 16)
                out[pl.ds(at, BS), :] = piece[:, d * LANES : (d + 1) * LANES].astype(jnp.bfloat16)
            at = pl.multiple_of(base + TAIL + j * HB, 16)
            out[pl.ds(at, HB), :] = pack_far(piece[:, FAR:], far_half(k)).astype(jnp.bfloat16)


def place_kernel(ny, ncol, rows, nb, slot_of, parts, mine, other, total, turned, placed):
    row = lax.axis_index("row")
    col = lax.axis_index("col")
    y, h = row // 2, row % 2
    per = NA // ncol
    sums = parts[0].astype(jnp.float32)
    for i in range(1, ncol):
        sums += parts[i].astype(jnp.float32) * (1.0 / (1.0 + i / ncol))
    total[...] = sums
    for d in range(ND - 1):
        tile = total[d * per * BS : (d + 1) * per * BS, :].T
        turned[d * LANES : (d + 1) * LANES, :] = tile * 0.5 if d == 0 else tile
    far = [unpack_far(total[TAIL + j * HB : TAIL + (j + 1) * HB, :]) for j in range(per)]
    turned[FAR:, :] = jnp.concatenate(far, axis=0).T
    placed[...] = jnp.zeros_like(placed)
    for j in range(per):
        index = find(slot_of, nb, col * per + j)

        @pl.when(index < KN)
        def _():
            group = index // GB
            for d in range(ND):
                to = lax.rem(group + d, NG)
                for b in range(GB if d < ND - 1 else GB // 2):
                    first = 0 if d < ND - 1 else far_half(index) * (GB // 2)
                    at = pl.multiple_of(slot_of[nb[0, to * GB + first + b]] * BS, BS)
                    r = d * LANES + b * BS
                    placed[pl.ds(at, BS), j * BS : (j + 1) * BS] = turned[
                        r : r + BS, j * BS : (j + 1) * BS
                    ]

    for shift in range(ny):
        owner = lax.rem(y + shift, ny)
        at = pl.multiple_of((2 * owner + h) * rows, 32)
        mine[shift] = placed[pl.ds(at, rows), :]
        at = pl.multiple_of((2 * owner + 1 - h) * rows, 32)
        other[shift] = placed[pl.ds(at, rows), :]


def mirror_kernel(part, direct, first, second, out):
    b = lax.axis_index("col") % 2
    for side, block in ((b, first), (1 - b, second)):
        at = pl.multiple_of(side * part, 32)
        out[pl.ds(at, part), :] = direct[pl.ds(at, part), :] + block[...].T


VMEM = pl.BlockSpec(memory_space=pltpu.VMEM)
SMEM = pl.BlockSpec(memory_space=pltpu.SMEM)
ANY = pl.BlockSpec(memory_space=pl.ANY)


def shards(three_center, density, neighbors, atom_slot):
    nrow = lax.axis_size("row")
    ncol = lax.axis_size("col")
    ny = nrow // 2
    rows, cols = density.shape
    total = NA * BS
    core = [(i, i ^ 1) for i in range(nrow)]

    def along(k):
        return [(i, (i + 2 * k) % nrow) for i in range(nrow)]

    pair = jnp.concatenate([density, lax.ppermute(density, "row", core)], axis=0)
    others = [lax.ppermute(pair, "row", along(k)) for k in range(1, ny)]
    block = pl.pallas_call(
        functools.partial(select_kernel, ny, ncol, rows),
        out_shape=jax.ShapeDtypeStruct((PANEL, LANES), jnp.bfloat16),
        in_specs=[SMEM, SMEM] + [ANY] * 4,
        out_specs=VMEM,
        scratch_shapes=[
            pltpu.VMEM((total, cols), jnp.bfloat16),
            pltpu.VMEM((WIDTH, LANES), jnp.bfloat16),
            pltpu.VMEM((LANES, WIDTH + KEEP - LANES), jnp.bfloat16),
            pltpu.SemaphoreType.DMA((2 * ny,)),
        ],
        compiler_params=params(12),
        name="select",
    )(neighbors, atom_slot, pair, *others)
    side = math.isqrt(ncol)

    def stage(k, first):
        pairs = []
        for r in range(nrow):
            for c in range(ncol):
                z, x = divmod(c, side)
                if (r % 2 == 0) == first:
                    x = (x + k) % side
                else:
                    z = (z + k) % side
                pairs.append((r * ncol + c, r * ncol + z * side + x))
        return pairs

    both = ("row", "col")
    line = [block] + [lax.ppermute(block, both, stage(k, True)) for k in range(1, side)]
    line = jnp.concatenate(line, axis=0)
    plane = [line] + [lax.ppermute(line, both, stage(k, False)) for k in range(1, side)]
    tensor = three_center[0]
    nfun = tensor.shape[0]
    sent = pl.pallas_call(
        functools.partial(exchange_kernel, side),
        out_shape=jax.ShapeDtypeStruct((ncol * PANEL, LANES), jnp.bfloat16),
        grid=(nfun,),
        in_specs=[pl.BlockSpec(line.shape, lambda p: (0, 0))] * side
        + [
            SMEM,
            SMEM,
            pl.BlockSpec((1, WIDTH, WIDTH), lambda p: (p, 0, 0)),
        ],
        out_specs=pl.BlockSpec((ncol * PANEL, LANES), lambda p: (0, 0)),
        scratch_shapes=[
            pltpu.VMEM((ncol * PANEL, LANES), jnp.bfloat16),
            pltpu.VMEM((WIDTH, WIDTH), jnp.bfloat16),
            pltpu.VMEM((WIDTH, WIDTH), jnp.bfloat16),
            pltpu.VMEM((4, 2 * LANES, 6 * LANES), jnp.float32),
        ],
        compiler_params=params(48),
        name="exchange",
    )(*plane, neighbors, atom_slot, tensor)
    parts = lax.all_to_all(sent.reshape(ncol, PANEL, LANES), "col", 0, 0, tiled=True)
    mine, other = pl.pallas_call(
        functools.partial(place_kernel, ny, ncol, rows),
        out_shape=[jax.ShapeDtypeStruct((ny, rows, cols), jnp.float32)] * 2,
        in_specs=[SMEM, SMEM, VMEM],
        out_specs=[VMEM, VMEM],
        scratch_shapes=[
            pltpu.VMEM((PANEL, LANES), jnp.float32),
            pltpu.VMEM((KEEP, cols), jnp.float32),
            pltpu.VMEM((total, cols), jnp.float32),
        ],
        compiler_params=params(12),
        name="place",
    )(neighbors, atom_slot, parts)
    chip = mine + lax.ppermute(other, "row", core)
    direct = chip[0]
    for k in range(1, ny):
        direct = direct + lax.ppermute(chip[k], "row", along(k))
    half = rows // 2
    b = lax.axis_index("col") % 2
    same = [(R * ncol + C, (C // 2) * ncol + 2 * R + C % 2) for R in range(nrow) for C in range(ncol)]
    swap = [(R * ncol + C, (C // 2) * ncol + 2 * R + 1 - C % 2) for R in range(nrow) for C in range(ncol)]
    upper, lower = direct[:half], direct[half:]
    first = lax.ppermute(jnp.where(b == 0, upper, lower), ("row", "col"), same)
    second = lax.ppermute(jnp.where(b == 0, lower, upper), ("row", "col"), swap)
    return pl.pallas_call(
        functools.partial(mirror_kernel, half),
        out_shape=jax.ShapeDtypeStruct((rows, cols), jnp.float32),
        in_specs=[VMEM] * 3,
        out_specs=VMEM,
        compiler_params=params(12),
        name="mirror",
    )(direct, first, second)


def solution(mesh):
    placed = (P("row", "col", None, None), P("row", "col"), P("row", None), P())
    return jax.shard_map(
        shards, mesh=mesh, in_specs=placed, out_specs=P("row", "col"), check_vma=False
    )
```

```python
import functools
import math

import jax
import jax.numpy as jnp
from jax import lax
from jax.experimental import pallas as pl
from jax.experimental.pallas import tpu as pltpu
from jax.sharding import PartitionSpec as P

BS = 32
KN = 32
NA = 48
LANES = 128
GB = LANES // BS
NG = KN // GB
ND = NG // 2 + 1
WIDTH = KN * BS
KEEP = ND * LANES
FAR = (ND - 1) * LANES
HB = BS // 2
PANEL = 3 * (BS * (ND - 1) + HB)
TAIL = 3 * BS * (ND - 1)
MIB = 1 << 20


def params(mib):
    return pltpu.CompilerParams(vmem_limit_bytes=mib * MIB)


def find(table, storage):
    index = jnp.int32(KN)
    for k in range(KN):
        index = jnp.where(table[KN + table[k]] == storage, k, index)
    return index


def far_half(index):
    late = (index // (KN // 2)) % 2
    upper = (index % GB) // (GB // 2)
    return (upper + late) % 2


def pack_far(tile, half):
    turn = pltpu.roll(tile, LANES // 2, 1)
    left = lax.broadcasted_iota(jnp.int32, (HB, LANES), 1) < LANES // 2
    low = jnp.where(half == 0, tile, turn)[:HB]
    high = jnp.where(half == 0, turn, tile)[HB:]
    return jnp.where(left, low, high)


def unpack_far(packed):
    return jnp.concatenate([packed, pltpu.roll(packed, LANES // 2, 1)], axis=0)


def select_kernel(ny, ncol, rows, table, p0, p1, p2, p3, out, panel, chosen, turned, sem):
    row = lax.axis_index("row")
    col = lax.axis_index("col")
    y, h = row // 2, row % 2
    copies = []
    for shift, part in enumerate((p0, p1, p2, p3)):
        owner = lax.rem(y - shift + ny, ny)
        for side in range(2):
            at = pl.multiple_of((2 * owner + (h if side == 0 else 1 - h)) * rows, 32)
            copies.append(
                pltpu.make_async_copy(
                    part.at[pl.ds(side * rows, rows), :],
                    panel.at[pl.ds(at, rows), :],
                    sem.at[2 * shift + side],
                )
            )
    for copy in copies:
        copy.start()
    for copy in copies:
        copy.wait()
    for k in range(KN):
        at = pl.multiple_of(table[KN + table[k]] * BS, BS)
        chosen[k * BS : (k + 1) * BS, :96] = panel[pl.ds(at, BS), :]
    for i in range(NG):
        tile = chosen[i * LANES : (i + 1) * LANES, :].T
        turned[:, i * LANES : (i + 1) * LANES] = tile
        if i < ND - 1:
            turned[:, (NG + i) * LANES : (NG + i + 1) * LANES] = tile
    per = NA // ncol
    for j in range(per):
        index = find(table, col * per + j)
        group = jnp.where(index < KN, index // GB, 0)
        start = pl.multiple_of(group * LANES, LANES)
        lines = turned[j * BS : (j + 1) * BS, pl.ds(start, KEEP)]
        for d in range(ND - 1):
            r = (d * per + j) * BS
            out[r : r + BS, :] = lines[:, d * LANES : (d + 1) * LANES]
        far = pack_far(lines[:, FAR:].astype(jnp.float32), far_half(index))
        out[TAIL + j * HB : TAIL + (j + 1) * HB, :] = far.astype(jnp.bfloat16)


def place_of(storage):
    return (storage // 3) * PANEL, storage % 3


def exchange_kernel(side, q0, q1, q2, q3, table, tensor, out, gathered, local, half, acc):
    step = pl.program_id(0)
    big = 2 * LANES
    tiles = WIDTH // big

    @pl.when(step == 0)
    def _():
        h = lax.axis_index("row") % 2
        z, x = lax.axis_index("col") // side, lax.axis_index("col") % side
        left = lax.broadcasted_iota(jnp.int32, (BS, LANES), 1) < LANES // 2
        for j, part in enumerate((q0, q1, q2, q3)):
            for k in range(side):
                dz, dx = jnp.where(h == 0, j, k), jnp.where(h == 0, k, j)
                owner = lax.rem(z - dz + side, side) * side + lax.rem(x - dx + side, side)
                at = pl.multiple_of(owner * PANEL, 16)
                gathered[pl.ds(at, PANEL), :] = part[k * PANEL : (k + 1) * PANEL, :]
        for k in range(KN):
            base, j = place_of(table[KN + table[k]])
            group = k // GB
            for d in range(ND - 1):
                to = (group + d) % NG
                at = pl.multiple_of(base + (d * 3 + j) * BS, 16)
                local[k * BS : (k + 1) * BS, to * LANES : (to + 1) * LANES] = gathered[pl.ds(at, BS), :]
            at = pl.multiple_of(base + TAIL + j * HB, 16)
            tile = unpack_far(gathered[pl.ds(at, HB), :].astype(jnp.float32))
            if far_half(k):
                tile = jnp.where(left, 0.0, pltpu.roll(tile, LANES // 2, 1))
            else:
                tile = jnp.where(left, tile, 0.0)
            to = (group + NG // 2) % NG
            local[k * BS : (k + 1) * BS, to * LANES : (to + 1) * LANES] = tile.astype(jnp.bfloat16)
        for group in range(NG):
            here = slice(group * LANES, (group + 1) * LANES)
            for d in range(1, NG // 2):
                to = (group + d) % NG
                there = slice(to * LANES, (to + 1) * LANES)
                local[there, here] = local[here, there].T
        for group in range(NG // 2):
            here = slice(group * LANES, (group + 1) * LANES)
            there = slice((group + NG // 2) * LANES, (group + NG // 2 + 1) * LANES)
            tile = local[here, there] + local[there, here].T
            local[here, there] = tile
            local[there, here] = tile.T
        acc[...] = jnp.zeros_like(acc)

    for i in range(tiles):
        half[i * big : (i + 1) * big, :] = jnp.dot(
            local[i * big : (i + 1) * big, :], tensor[0], preferred_element_type=jnp.float32
        ).astype(jnp.bfloat16)
    for i in range(tiles):
        left = tensor[0, i * big : (i + 1) * big, :]
        first, second = ((tiles - 1, 0), (tiles - 1, 0), (2, 0), (1, 1))[i]
        acc[i, :, : first * big] += jnp.dot(
            left, half[:, i * big : (i + first) * big], preferred_element_type=jnp.float32
        )
        if second:
            acc[i, :, first * big : (first + second) * big] += jnp.dot(
                left, half[:, : second * big], preferred_element_type=jnp.float32
            )

    @pl.when(step == pl.num_programs(0) - 1)
    def _():
        ncol = lax.axis_size("col")
        scale = 1.0 + lax.axis_index("col").astype(jnp.float32) / ncol
        out[...] = jnp.zeros_like(out)
        for i in range(tiles // 2):
            acc[i + tiles // 2, :, 2 * big :] = acc[i, :, 2 * big :].T
        for k in range(KN):
            base, j = place_of(table[KN + table[k]])
            group = k // GB
            i, odd = group // 2, group % 2
            r = (k % (2 * GB)) * BS
            piece = acc[i, r : r + BS, odd * LANES : odd * LANES + KEEP] * scale
            for d in range(ND - 1):
                at = pl.multiple_of(base + (d * 3 + j) * BS, 16)
                out[pl.ds(at, BS), :] = piece[:, d * LANES : (d + 1) * LANES].astype(jnp.bfloat16)
            at = pl.multiple_of(base + TAIL + j * HB, 16)
            out[pl.ds(at, HB), :] = pack_far(piece[:, FAR:], far_half(k)).astype(jnp.bfloat16)


def place_kernel(ny, ncol, rows, table, parts, mine, other, total, turned, placed):
    row = lax.axis_index("row")
    col = lax.axis_index("col")
    y, h = row // 2, row % 2
    per = NA // ncol
    sums = parts[0].astype(jnp.float32)
    for i in range(1, ncol):
        sums += parts[i].astype(jnp.float32) * (1.0 / (1.0 + i / ncol))
    total[...] = sums
    for d in range(ND - 1):
        tile = total[d * per * BS : (d + 1) * per * BS, :].T
        turned[d * LANES : (d + 1) * LANES, :] = tile * 0.5 if d == 0 else tile
    far = [unpack_far(total[TAIL + j * HB : TAIL + (j + 1) * HB, :]) for j in range(per)]
    turned[FAR:, :] = jnp.concatenate(far, axis=0).T
    placed[...] = jnp.zeros_like(placed)
    for j in range(per):
        index = find(table, col * per + j)

        @pl.when(index < KN)
        def _():
            group = index // GB
            for d in range(ND):
                to = lax.rem(group + d, NG)
                for b in range(GB if d < ND - 1 else GB // 2):
                    first = 0 if d < ND - 1 else far_half(index) * (GB // 2)
                    at = pl.multiple_of(table[KN + table[to * GB + first + b]] * BS, BS)
                    r = d * LANES + b * BS
                    placed[pl.ds(at, BS), j * BS : (j + 1) * BS] = turned[
                        r : r + BS, j * BS : (j + 1) * BS
                    ]

    for shift in range(ny):
        owner = lax.rem(y + shift, ny)
        at = pl.multiple_of((2 * owner + h) * rows, 32)
        mine[shift] = placed[pl.ds(at, rows), :]
        at = pl.multiple_of((2 * owner + 1 - h) * rows, 32)
        other[shift] = placed[pl.ds(at, rows), :]


def mirror_kernel(part, direct, first, second, out):
    b = lax.axis_index("col") % 2
    for side, block in ((b, first), (1 - b, second)):
        at = pl.multiple_of(side * part, 32)
        out[pl.ds(at, part), :] = direct[pl.ds(at, part), :] + block[...].T


VMEM = pl.BlockSpec(memory_space=pltpu.VMEM)
SMEM = pl.BlockSpec(memory_space=pltpu.SMEM)
ANY = pl.BlockSpec(memory_space=pl.ANY)


def shards(three_center, density, neighbors, atom_slot):
    nrow = lax.axis_size("row")
    ncol = lax.axis_size("col")
    ny = nrow // 2
    rows, cols = density.shape
    total = NA * BS
    core = [(i, i ^ 1) for i in range(nrow)]

    def along(k):
        return [(i, (i + 2 * k) % nrow) for i in range(nrow)]

    table = jnp.concatenate([neighbors[0], atom_slot])
    pair = jnp.concatenate([density, lax.ppermute(density, "row", core)], axis=0)
    others = [lax.ppermute(pair, "row", along(k)) for k in range(1, ny)]
    block = pl.pallas_call(
        functools.partial(select_kernel, ny, ncol, rows),
        out_shape=jax.ShapeDtypeStruct((PANEL, LANES), jnp.bfloat16),
        in_specs=[SMEM] + [ANY] * 4,
        out_specs=VMEM,
        scratch_shapes=[
            pltpu.VMEM((total, cols), jnp.bfloat16),
            pltpu.VMEM((WIDTH, LANES), jnp.bfloat16),
            pltpu.VMEM((LANES, WIDTH + KEEP - LANES), jnp.bfloat16),
            pltpu.SemaphoreType.DMA((2 * ny,)),
        ],
        compiler_params=params(12),
        name="select",
    )(table, pair, *others)
    side = math.isqrt(ncol)

    def stage(k, first):
        pairs = []
        for r in range(nrow):
            for c in range(ncol):
                z, x = divmod(c, side)
                if (r % 2 == 0) == first:
                    x = (x + k) % side
                else:
                    z = (z + k) % side
                pairs.append((r * ncol + c, r * ncol + z * side + x))
        return pairs

    both = ("row", "col")
    line = [block] + [lax.ppermute(block, both, stage(k, True)) for k in range(1, side)]
    line = jnp.concatenate(line, axis=0)
    plane = [line] + [lax.ppermute(line, both, stage(k, False)) for k in range(1, side)]
    tensor = three_center[0]
    nfun = tensor.shape[0]
    sent = pl.pallas_call(
        functools.partial(exchange_kernel, side),
        out_shape=jax.ShapeDtypeStruct((ncol * PANEL, LANES), jnp.bfloat16),
        grid=(nfun,),
        in_specs=[pl.BlockSpec(line.shape, lambda p: (0, 0))] * side
        + [
            SMEM,
            pl.BlockSpec((1, WIDTH, WIDTH), lambda p: (p, 0, 0)),
        ],
        out_specs=pl.BlockSpec((ncol * PANEL, LANES), lambda p: (0, 0)),
        scratch_shapes=[
            pltpu.VMEM((ncol * PANEL, LANES), jnp.bfloat16),
            pltpu.VMEM((WIDTH, WIDTH), jnp.bfloat16),
            pltpu.VMEM((WIDTH, WIDTH), jnp.bfloat16),
            pltpu.VMEM((4, 2 * LANES, 6 * LANES), jnp.float32),
        ],
        compiler_params=params(48),
        name="exchange",
    )(*plane, table, tensor)
    parts = lax.all_to_all(sent.reshape(ncol, PANEL, LANES), "col", 0, 0, tiled=True)
    mine, other = pl.pallas_call(
        functools.partial(place_kernel, ny, ncol, rows),
        out_shape=[jax.ShapeDtypeStruct((ny, rows, cols), jnp.float32)] * 2,
        in_specs=[SMEM, VMEM],
        out_specs=[VMEM, VMEM],
        scratch_shapes=[
            pltpu.VMEM((PANEL, LANES), jnp.float32),
            pltpu.VMEM((KEEP, cols), jnp.float32),
            pltpu.VMEM((total, cols), jnp.float32),
        ],
        compiler_params=params(12),
        name="place",
    )(table, parts)
    chip = mine + lax.ppermute(other, "row", core)
    direct = chip[0]
    for k in range(1, ny):
        direct = direct + lax.ppermute(chip[k], "row", along(k))
    half = rows // 2
    b = lax.axis_index("col") % 2
    same = [(R * ncol + C, (C // 2) * ncol + 2 * R + C % 2) for R in range(nrow) for C in range(ncol)]
    swap = [(R * ncol + C, (C // 2) * ncol + 2 * R + 1 - C % 2) for R in range(nrow) for C in range(ncol)]
    upper, lower = direct[:half], direct[half:]
    first = lax.ppermute(jnp.where(b == 0, upper, lower), ("row", "col"), same)
    second = lax.ppermute(jnp.where(b == 0, lower, upper), ("row", "col"), swap)
    return pl.pallas_call(
        functools.partial(mirror_kernel, half),
        out_shape=jax.ShapeDtypeStruct((rows, cols), jnp.float32),
        in_specs=[VMEM] * 3,
        out_specs=VMEM,
        compiler_params=params(12),
        name="mirror",
    )(direct, first, second)


def solution(mesh):
    placed = (P("row", "col", None, None), P("row", "col"), P("row", None), P())
    return jax.shard_map(
        shards, mesh=mesh, in_specs=placed, out_specs=P("row", "col"), check_vma=False
    )
```

```python
import functools
import math

import jax
import jax.numpy as jnp
from jax import lax
from jax.experimental import pallas as pl
from jax.experimental.pallas import tpu as pltpu
from jax.sharding import PartitionSpec as P

BS = 32
KN = 32
NA = 48
LANES = 128
GB = LANES // BS
NG = KN // GB
ND = NG // 2 + 1
WIDTH = KN * BS
KEEP = ND * LANES
FAR = (ND - 1) * LANES
HB = BS // 2
PANEL = 3 * (BS * (ND - 1) + HB)
TAIL = 3 * BS * (ND - 1)
MIB = 1 << 20


def params(mib):
    return pltpu.CompilerParams(vmem_limit_bytes=mib * MIB)


def find(table, storage):
    index = jnp.int32(KN)
    for k in range(KN):
        index = jnp.where(table[KN + table[k]] == storage, k, index)
    return index


def far_half(index):
    late = (index // (KN // 2)) % 2
    upper = (index % GB) // (GB // 2)
    return (upper + late) % 2


def pack_far(tile, half):
    turn = pltpu.roll(tile, LANES // 2, 1)
    left = lax.broadcasted_iota(jnp.int32, (HB, LANES), 1) < LANES // 2
    low = jnp.where(half == 0, tile, turn)[:HB]
    high = jnp.where(half == 0, turn, tile)[HB:]
    return jnp.where(left, low, high)


def unpack_far(packed):
    return jnp.concatenate([packed, pltpu.roll(packed, LANES // 2, 1)], axis=0)


def select_kernel(ny, ncol, rows, table, p0, p1, p2, p3, out, panel, chosen, turned, sem):
    row = lax.axis_index("row")
    col = lax.axis_index("col")
    y, h = row // 2, row % 2
    copies = []
    for shift, part in zip((0,) + SHIFTS, (p0, p1, p2, p3)):
        owner = lax.rem(y - shift + ny, ny)
        for side in range(2):
            at = pl.multiple_of((2 * owner + (h if side == 0 else 1 - h)) * rows, 32)
            copies.append(
                pltpu.make_async_copy(
                    part.at[pl.ds(side * rows, rows), :],
                    panel.at[pl.ds(at, rows), :],
                    sem.at[2 * shift + side],
                )
            )
    for copy in copies:
        copy.start()
    for copy in copies:
        copy.wait()
    for k in range(KN):
        at = pl.multiple_of(table[KN + table[k]] * BS, BS)
        chosen[k * BS : (k + 1) * BS, :96] = panel[pl.ds(at, BS), :]
    for i in range(NG):
        tile = chosen[i * LANES : (i + 1) * LANES, :].T
        turned[:, i * LANES : (i + 1) * LANES] = tile
        if i < ND - 1:
            turned[:, (NG + i) * LANES : (NG + i + 1) * LANES] = tile
    per = NA // ncol
    for j in range(per):
        index = find(table, col * per + j)
        group = jnp.where(index < KN, index // GB, 0)
        start = pl.multiple_of(group * LANES, LANES)
        lines = turned[j * BS : (j + 1) * BS, pl.ds(start, KEEP)]
        for d in range(ND - 1):
            r = (d * per + j) * BS
            out[r : r + BS, :] = lines[:, d * LANES : (d + 1) * LANES]
        far = pack_far(lines[:, FAR:].astype(jnp.float32), far_half(index))
        out[TAIL + j * HB : TAIL + (j + 1) * HB, :] = far.astype(jnp.bfloat16)


def place_of(storage):
    return (storage // 3) * PANEL, storage % 3


def exchange_kernel(side, q0, q1, q2, q3, table, tensor, out, gathered, local, half, acc, fetched, sem):
    nfun = tensor.shape[0]
    big = 2 * LANES
    tiles = WIDTH // big

    def fetch(p):
        return pltpu.make_async_copy(tensor.at[p], fetched.at[p % 3], sem.at[p])

    def first_product(p):
        half[p % 2] = jnp.dot(
            local[...], fetched[p % 3], preferred_element_type=jnp.float32
        ).astype(jnp.bfloat16)

    def second_product(p):
        for i in range(tiles):
            left = fetched[p % 3, i * big : (i + 1) * big, :]
            first, second = ((tiles - 1, 0), (tiles - 1, 0), (2, 0), (1, 1))[i]
            acc[i, :, : first * big] += jnp.dot(
                left, half[p % 2, :, i * big : (i + first) * big], preferred_element_type=jnp.float32
            )
            if second:
                acc[i, :, first * big : (first + second) * big] += jnp.dot(
                    left, half[p % 2, :, : second * big], preferred_element_type=jnp.float32
                )

    fetch(0).start()
    h = lax.axis_index("row") % 2
    z, x = lax.axis_index("col") // side, lax.axis_index("col") % side
    left = lax.broadcasted_iota(jnp.int32, (BS, LANES), 1) < LANES // 2
    for j, part in zip((0,) + SHIFTS, (q0, q1, q2, q3)):
        for i, k in enumerate((0,) + SHIFTS):
            dz, dx = jnp.where(h == 0, j, k), jnp.where(h == 0, k, j)
            owner = lax.rem(z - dz + side, side) * side + lax.rem(x - dx + side, side)
            at = pl.multiple_of(owner * PANEL, 16)
            gathered[pl.ds(at, PANEL), :] = part[i * PANEL : (i + 1) * PANEL, :]
    for k in range(KN):
        base, j = place_of(table[KN + table[k]])
        group = k // GB
        for d in range(ND - 1):
            to = (group + d) % NG
            at = pl.multiple_of(base + (d * 3 + j) * BS, 16)
            local[k * BS : (k + 1) * BS, to * LANES : (to + 1) * LANES] = gathered[pl.ds(at, BS), :]
        at = pl.multiple_of(base + TAIL + j * HB, 16)
        tile = unpack_far(gathered[pl.ds(at, HB), :].astype(jnp.float32))
        if far_half(k):
            tile = jnp.where(left, 0.0, pltpu.roll(tile, LANES // 2, 1))
        else:
            tile = jnp.where(left, tile, 0.0)
        to = (group + NG // 2) % NG
        local[k * BS : (k + 1) * BS, to * LANES : (to + 1) * LANES] = tile.astype(jnp.bfloat16)
    for group in range(NG):
        here = slice(group * LANES, (group + 1) * LANES)
        for d in range(1, NG // 2):
            to = (group + d) % NG
            there = slice(to * LANES, (to + 1) * LANES)
            local[there, here] = local[here, there].T
    for group in range(NG // 2):
        here = slice(group * LANES, (group + 1) * LANES)
        there = slice((group + NG // 2) * LANES, (group + NG // 2 + 1) * LANES)
        tile = local[here, there] + local[there, here].T
        local[here, there] = tile
        local[there, here] = tile.T
    acc[...] = jnp.zeros_like(acc)
    fetch(1).start()
    fetch(0).wait()
    first_product(0)
    for p in range(nfun):
        if p + 2 < nfun:
            fetch(p + 2).start()
        if p + 1 < nfun:
            fetch(p + 1).wait()
            first_product(p + 1)
        second_product(p)

    ncol = lax.axis_size("col")
    scale = 1.0 + lax.axis_index("col").astype(jnp.float32) / ncol
    out[...] = jnp.zeros_like(out)
    for i in range(tiles // 2):
        acc[i + tiles // 2, :, 2 * big :] = acc[i, :, 2 * big :].T
    for k in range(KN):
        base, j = place_of(table[KN + table[k]])
        group = k // GB
        i, odd = group // 2, group % 2
        r = (k % (2 * GB)) * BS
        piece = acc[i, r : r + BS, odd * LANES : odd * LANES + KEEP] * scale
        for d in range(ND - 1):
            at = pl.multiple_of(base + (d * 3 + j) * BS, 16)
            out[pl.ds(at, BS), :] = piece[:, d * LANES : (d + 1) * LANES].astype(jnp.bfloat16)
        at = pl.multiple_of(base + TAIL + j * HB, 16)
        out[pl.ds(at, HB), :] = pack_far(piece[:, FAR:], far_half(k)).astype(jnp.bfloat16)


def place_kernel(ny, ncol, rows, table, parts, mine, other, total, turned, placed):
    row = lax.axis_index("row")
    col = lax.axis_index("col")
    y, h = row // 2, row % 2
    per = NA // ncol
    sums = parts[0].astype(jnp.float32)
    for i in range(1, ncol):
        sums += parts[i].astype(jnp.float32) * (1.0 / (1.0 + i / ncol))
    total[...] = sums
    for d in range(ND - 1):
        tile = total[d * per * BS : (d + 1) * per * BS, :].T
        turned[d * LANES : (d + 1) * LANES, :] = tile * 0.5 if d == 0 else tile
    far = [unpack_far(total[TAIL + j * HB : TAIL + (j + 1) * HB, :]) for j in range(per)]
    turned[FAR:, :] = jnp.concatenate(far, axis=0).T
    placed[...] = jnp.zeros_like(placed)
    for j in range(per):
        index = find(table, col * per + j)

        @pl.when(index < KN)
        def _():
            group = index // GB
            for d in range(ND):
                to = lax.rem(group + d, NG)
                for b in range(GB if d < ND - 1 else GB // 2):
                    first = 0 if d < ND - 1 else far_half(index) * (GB // 2)
                    at = pl.multiple_of(table[KN + table[to * GB + first + b]] * BS, BS)
                    r = d * LANES + b * BS
                    placed[pl.ds(at, BS), j * BS : (j + 1) * BS] = turned[
                        r : r + BS, j * BS : (j + 1) * BS
                    ]

    for shift in range(ny):
        owner = lax.rem(y + shift, ny)
        at = pl.multiple_of((2 * owner + h) * rows, 32)
        mine[shift] = placed[pl.ds(at, rows), :]
        at = pl.multiple_of((2 * owner + 1 - h) * rows, 32)
        other[shift] = placed[pl.ds(at, rows), :]


def mirror_kernel(part, direct, first, second, out):
    b = lax.axis_index("col") % 2
    for side, block in ((b, first), (1 - b, second)):
        at = pl.multiple_of(side * part, 32)
        out[pl.ds(at, part), :] = direct[pl.ds(at, part), :] + block[...].T


SHIFTS = (2, 1, 3)


VMEM = pl.BlockSpec(memory_space=pltpu.VMEM)
SMEM = pl.BlockSpec(memory_space=pltpu.SMEM)
ANY = pl.BlockSpec(memory_space=pl.ANY)


def shards(three_center, density, neighbors, atom_slot):
    nrow = lax.axis_size("row")
    ncol = lax.axis_size("col")
    ny = nrow // 2
    rows, cols = density.shape
    total = NA * BS
    core = [(i, i ^ 1) for i in range(nrow)]

    def along(k):
        return [(i, (i + 2 * k) % nrow) for i in range(nrow)]

    table = jnp.concatenate([neighbors[0], atom_slot])
    pair = jnp.concatenate([density, lax.ppermute(density, "row", core)], axis=0)
    others = [lax.ppermute(pair, "row", along(k)) for k in SHIFTS]
    block = pl.pallas_call(
        functools.partial(select_kernel, ny, ncol, rows),
        out_shape=jax.ShapeDtypeStruct((PANEL, LANES), jnp.bfloat16),
        in_specs=[SMEM] + [ANY] * 4,
        out_specs=VMEM,
        scratch_shapes=[
            pltpu.VMEM((total, cols), jnp.bfloat16),
            pltpu.VMEM((WIDTH, LANES), jnp.bfloat16),
            pltpu.VMEM((LANES, WIDTH + KEEP - LANES), jnp.bfloat16),
            pltpu.SemaphoreType.DMA((2 * ny,)),
        ],
        compiler_params=params(12),
        name="select",
    )(table, pair, *others)
    side = math.isqrt(ncol)

    def stage(k, first):
        pairs = []
        for r in range(nrow):
            for c in range(ncol):
                z, x = divmod(c, side)
                if (r % 2 == 0) == first:
                    x = (x + k) % side
                else:
                    z = (z + k) % side
                pairs.append((r * ncol + c, r * ncol + z * side + x))
        return pairs

    both = ("row", "col")
    line = [block] + [lax.ppermute(block, both, stage(k, True)) for k in SHIFTS]
    line = jnp.concatenate(line, axis=0)
    plane = [line] + [lax.ppermute(line, both, stage(k, False)) for k in SHIFTS]
    tensor = three_center[0]
    nfun = tensor.shape[0]
    sent = pl.pallas_call(
        functools.partial(exchange_kernel, side),
        out_shape=jax.ShapeDtypeStruct((ncol * PANEL, LANES), jnp.bfloat16),
        in_specs=[VMEM] * side + [SMEM, ANY],
        out_specs=VMEM,
        scratch_shapes=[
            pltpu.VMEM((ncol * PANEL, LANES), jnp.bfloat16),
            pltpu.VMEM((WIDTH, WIDTH), jnp.bfloat16),
            pltpu.VMEM((2, WIDTH, WIDTH), jnp.bfloat16),
            pltpu.VMEM((4, 2 * LANES, 6 * LANES), jnp.float32),
            pltpu.VMEM((3, WIDTH, WIDTH), jnp.bfloat16),
            pltpu.SemaphoreType.DMA((nfun,)),
        ],
        compiler_params=params(48),
        name="exchange",
    )(*plane, table, tensor)
    parts = lax.all_to_all(sent.reshape(ncol, PANEL, LANES), "col", 0, 0, tiled=True)
    mine, other = pl.pallas_call(
        functools.partial(place_kernel, ny, ncol, rows),
        out_shape=[jax.ShapeDtypeStruct((ny, rows, cols), jnp.float32)] * 2,
        in_specs=[SMEM, VMEM],
        out_specs=[VMEM, VMEM],
        scratch_shapes=[
            pltpu.VMEM((PANEL, LANES), jnp.float32),
            pltpu.VMEM((KEEP, cols), jnp.float32),
            pltpu.VMEM((total, cols), jnp.float32),
        ],
        compiler_params=params(12),
        name="place",
    )(table, parts)
    chip = mine + lax.ppermute(other, "row", core)
    direct = chip[0]
    for k in SHIFTS:
        direct = direct + lax.ppermute(chip[k], "row", along(k))
    half = rows // 2
    b = lax.axis_index("col") % 2
    same = [(R * ncol + C, (C // 2) * ncol + 2 * R + C % 2) for R in range(nrow) for C in range(ncol)]
    swap = [(R * ncol + C, (C // 2) * ncol + 2 * R + 1 - C % 2) for R in range(nrow) for C in range(ncol)]
    upper, lower = direct[:half], direct[half:]
    first = lax.ppermute(jnp.where(b == 0, upper, lower), ("row", "col"), same)
    second = lax.ppermute(jnp.where(b == 0, lower, upper), ("row", "col"), swap)
    return pl.pallas_call(
        functools.partial(mirror_kernel, half),
        out_shape=jax.ShapeDtypeStruct((rows, cols), jnp.float32),
        in_specs=[VMEM] * 3,
        out_specs=VMEM,
        compiler_params=params(12),
        name="mirror",
    )(direct, first, second)


def solution(mesh):
    placed = (P("row", "col", None, None), P("row", "col"), P("row", None), P())
    return jax.shard_map(
        shards, mesh=mesh, in_specs=placed, out_specs=P("row", "col"), check_vma=False
    )
```
